32 devices in a mesh: node: 16 (over z, x, core), local: 2 (over y).
Axes of the slice: x: 2, y: 2, z: 4, core: 2. Of those that a mesh axis runs over, the one named last changes fastest.
Arguments:
- master_weight: bfloat16 [64, 128, 2048], P(None, 'node', 'local'), may hold values from -6 to 6
- first_moment: float32 [64, 128, 2048], P(None, 'node', 'local'), may hold values from -6 to 6
- second_moment: float32 [64, 128, 2048], P(None, 'node', 'local'), may hold values from 0.25 to 4
- features: bfloat16 [96, 2, 128, 128], P('node', 'local'), may hold values from -6 to 6
- grad_out: bfloat16 [96, 2, 128, 2048], P('node', 'local'), may hold values from -0.375 to 0.375
- old_place: int32 [80], replicated, may hold values from 0 to 95, as said below
- new_place: int32 [80], replicated, may hold values from 0 to 95, as said below
- old_owner: int32 [16], replicated, may hold values from 0 to 63
- new_owner: int32 [16], replicated, may hold values from 0 to 63
Outputs:
- slot_weight: bfloat16 [96, 128, 2048], P('node', None, 'local')
- slot_first: float32 [96, 128, 2048], P('node', None, 'local')
- slot_second: float32 [96, 128, 2048], P('node', None, 'local')
The draws below stay inside these ranges and needn't reach their ends.
Inputs may be any that keep to these rules, and one draw needn't show every extreme that they name: `old_place`: 80 distinct positions; position p belongs to node p // 6; in every draw some node has all 6 of its positions taken. `new_place`: 80 distinct positions; position p belongs to node p // 6; in every draw some node has all 6 of its positions taken.
All inputs are finite; a program needn't handle non-finite values.
Results may differ from the reference program's by a relative error of at most 0.0044.
Values may be sent and summed in bfloat16 or wider, within the bound.
No kernel may reach another device: no remote copies, remote signals or barrier semaphores. Data moves between devices by JAX's collectives and lax.ppermute only.
A program may use at most 64 MiB of HBM per device.

```python
import math
import jax
import jax.numpy as jnp
from jax import lax

EXPERTS = 64
REDUNDANT = 16
FF = 2048
ROWS = 128
TOK = 128
SLOTS = 80
CAP = 6
POSITIONS = 96
N_NODE = 16
N_LOCAL = 2


def place_draw(key):
    node_key, rest_key, order_key = jax.random.split(key, 3)
    full_node = jax.random.randint(node_key, (), 0, N_NODE).astype(jnp.int32)
    others = jax.random.permutation(rest_key, POSITIONS - CAP).astype(jnp.int32)
    others = jnp.where(others >= full_node * CAP, others + CAP, others)
    chosen = jnp.concatenate([full_node * CAP + jnp.arange(CAP, dtype=jnp.int32), others[:SLOTS - CAP]])
    order = jax.random.permutation(order_key, SLOTS)
    return chosen[order].astype(jnp.int32)


def draw_old_place(key, part):
    key = jax.random.fold_in(key, 11)
    return place_draw(key)


def draw_new_place(key, part):
    key = jax.random.fold_in(key, 23)
    return place_draw(key)


def set_ends(entries, stream_key, smallest, top_value):
    spot = [jax.random.randint(jax.random.fold_in(stream_key, axis), (), 0, length) for axis, length in enumerate(entries.shape)]
    longest = entries.shape.index(max(entries.shape))
    beside = spot[:longest] + [(spot[longest] + 1) % entries.shape[longest]] + spot[longest + 1:]
    return entries.at[tuple(spot)].set(smallest).at[tuple(beside)].set(top_value)


def steps_of(key, dims, shards, low, high):
    gain, own = 1.0, jax.random.fold_in(key, 6)
    for axis_at, parts in shards:
        heights = jnp.exp(jax.random.uniform(jax.random.fold_in(own, axis_at), (parts,), jnp.float32, low / len(shards), high / len(shards)))
        gain = gain * jnp.repeat(heights, dims[axis_at] // parts).reshape([-1 if axis == axis_at else 1 for axis in range(len(dims))])
    return gain


def bell_draw(rng, dims, width, most, pieces=(), held_as=jnp.bfloat16):
    array = width * jax.random.normal(rng, dims, jnp.float32)
    if pieces:
        array = array * steps_of(rng, dims, pieces, -0.22, 0.18)
    return jnp.clip(array, -most, most).astype(held_as)


def setup_inputs(seed: int = 0) -> dict:
    key_list = jax.random.split(jax.random.key(seed), 10)
    master_weight = bell_draw(key_list[0], (EXPERTS, ROWS, FF), 1.0, 6.0, ((1, 16), (2, 2)))
    first_moment = bell_draw(key_list[1], (EXPERTS, ROWS, FF), 1.0, 6.0, ((1, 16), (2, 2)), jnp.float32)
    second_moment = jnp.clip(jnp.exp(math.log(4.0) - 2.7725887 * jax.random.uniform(key_list[2], (EXPERTS, ROWS, FF), jnp.float32) ** steps_of(key_list[2], (EXPERTS, ROWS, FF), ((1, 16), (2, 2)), -0.2, 0.2)), 0.25, 4.0)
    features = bell_draw(key_list[3], (POSITIONS, N_LOCAL, TOK, ROWS), 1.0, 6.0, ((0, 16), (1, 2)))
    grad_out = bell_draw(key_list[4], (POSITIONS, N_LOCAL, TOK, FF), (TOK * N_LOCAL) ** -0.5, 0.375, ((0, 16), (1, 2)))
    old_place = draw_old_place(jax.random.fold_in(key_list[9], 71), 0)
    new_place = draw_new_place(jax.random.fold_in(key_list[9], 71), 0)
    old_owner = set_ends(jax.random.randint(key_list[7], (REDUNDANT,), 0, EXPERTS), jax.random.fold_in(key_list[7], 1), 0, EXPERTS - 1).astype(jnp.int32)
    new_owner = set_ends(jax.random.randint(key_list[8], (REDUNDANT,), 0, EXPERTS), jax.random.fold_in(key_list[8], 1), 0, EXPERTS - 1).astype(jnp.int32)
    return dict(master_weight=master_weight, first_moment=first_moment, second_moment=second_moment, features=features, grad_out=grad_out, old_place=old_place, new_place=new_place, old_owner=old_owner, new_owner=new_owner)


BETA_FIRST = 0.9
BETA_SECOND = 0.95
LEARNING_RATE = 0.1
DECAY_RATE = 0.1
EPSILON = 1e-08
CORRECT_FIRST = 1.0 - 0.9 ** 10
CORRECT_SECOND = 1.0 - 0.95 ** 10

def reference(master_weight, first_moment, second_moment, features, grad_out, old_place, new_place, old_owner, new_owner):
    primaries = jnp.arange(EXPERTS, dtype=jnp.int32)
    old_expert = jnp.concatenate([primaries, old_owner.astype(jnp.int32)])
    new_expert = jnp.concatenate([primaries, new_owner.astype(jnp.int32)])

    def slot_term(place):
        inputs = features[place].astype(jnp.float32)
        cotangent = grad_out[place].astype(jnp.float32)
        return jnp.einsum('ltr,ltf->rf', inputs, cotangent)
    slot_grad = lax.map(slot_term, old_place.astype(jnp.int32))
    gradient = jnp.zeros((EXPERTS, ROWS, FF), jnp.float32).at[old_expert].add(slot_grad)
    first_new = BETA_FIRST * first_moment + (1.0 - BETA_FIRST) * gradient
    second_new = BETA_SECOND * second_moment + (1.0 - BETA_SECOND) * gradient * gradient
    weight_old = master_weight.astype(jnp.float32)
    update = first_new / CORRECT_FIRST / (jnp.sqrt(second_new / CORRECT_SECOND) + EPSILON) + DECAY_RATE * weight_old
    weight_new = (weight_old - LEARNING_RATE * update).astype(jnp.bfloat16)
    holder = jnp.full((POSITIONS,), -1, jnp.int32).at[new_place.astype(jnp.int32)].set(new_expert)
    filled = (holder >= 0)[:, None, None]
    source = jnp.maximum(holder, 0)
    slot_weight = jnp.where(filled, weight_new[source], jnp.zeros((), jnp.bfloat16))
    slot_first = jnp.where(filled, first_new[source], jnp.zeros((), jnp.float32))
    slot_second = jnp.where(filled, second_new[source], jnp.zeros((), jnp.float32))
    return (slot_weight, slot_first, slot_second)
```

```python
import functools

import jax
import jax.numpy as jnp
from jax import lax
from jax.experimental import pallas as pl
from jax.experimental.pallas import tpu as pltpu
from jax.sharding import PartitionSpec as P

BETA_FIRST = 0.9
BETA_SECOND = 0.95
LEARNING_RATE = 0.1
DECAY_RATE = 0.1
EPSILON = 1e-08
CORRECT_FIRST = 1.0 - 0.9**10
CORRECT_SECOND = 1.0 - 0.95**10

VMEM_LIMIT = 64 * 1024 * 1024
SMALL_LIMIT = 28 * 1024 * 1024


def position_table(place, expert, positions, empty):
    match = place[:, None] == jnp.arange(positions, dtype=jnp.int32)[None, :]
    held = jnp.sum(jnp.where(match, expert[:, None] + 1, 0), axis=0)
    return jnp.where(held > 0, held - 1, empty).astype(jnp.int32)


def moments(first_moment, second_moment, gradient):
    first_new = BETA_FIRST * first_moment + (1.0 - BETA_FIRST) * gradient
    second_new = BETA_SECOND * second_moment + (1.0 - BETA_SECOND) * gradient * gradient
    return first_new, second_new


def step_weight(weight_old, first_new, second_new):
    scaled = second_new * (1.0 / CORRECT_SECOND)
    root = scaled * lax.rsqrt(jnp.maximum(scaled, 1e-37))
    update = first_new * (1.0 / CORRECT_FIRST) / (root + EPSILON) + DECAY_RATE * weight_old
    return weight_old - LEARNING_RATE * update


def pair_gradient(nodes, features_ref, grad_ref):
    rows = features_ref.shape[3] // nodes
    parts = []
    for side in range(2):
        product = lax.dot_general(
            features_ref[side, 0],
            grad_ref[side, 0],
            (((0,), (0,)), ((), ())),
            preferred_element_type=jnp.float32,
        )
        parts.append(product.reshape(nodes, rows, product.shape[1]))
    return jnp.concatenate(parts, axis=1)


def front_kernel(side_ref, place_ref, owner_ref, features_ref, grad_ref, weight_ref, ahead_ref, theirs_ref, table):
    nodes = ahead_ref.shape[0]
    experts = weight_ref.shape[0]
    pair = pl.program_id(0)
    pairs = pl.num_programs(0)

    @pl.when(pair == 0)
    def _():
        @pl.loop(0, table.shape[0], unroll=16)
        def _(position):
            table[position] = experts

        @pl.loop(0, experts, unroll=16)
        def _(expert):
            table[place_ref[expert]] = expert

        @pl.loop(0, owner_ref.shape[0], unroll=16)
        def _(slot):
            table[place_ref[experts + slot]] = owner_ref[slot]

    theirs_ref[:, 0] = pair_gradient(nodes, features_ref, grad_ref).astype(jnp.bfloat16)
    for node in range(nodes):
        both = []
        for side in range(2):
            expert = table[(node * pairs + pair) * 2 + side]
            held = weight_ref[jnp.minimum(expert, experts - 1)].astype(jnp.float32)
            both.append(jnp.where(expert < experts, held, 0.0))
        ahead_ref[node, 0] = jnp.concatenate(both, axis=0).astype(jnp.bfloat16)


def front_call(nodes, side, new_place, new_owner, features, grad_out, weight):
    capacity, _, tokens, rows = features.shape
    columns = weight.shape[2]
    pairs = capacity // 2
    shape = jax.ShapeDtypeStruct((nodes, pairs, 2 * rows // nodes, columns), jnp.bfloat16)
    block = pl.BlockSpec((nodes, 1) + shape.shape[2:], lambda i, *_: (0, i, 0, 0))
    return pl.pallas_call(
        front_kernel,
        out_shape=[shape, shape],
        grid_spec=pltpu.PrefetchScalarGridSpec(
            num_scalar_prefetch=3,
            grid=(pairs,),
            in_specs=[
                pl.BlockSpec((2, 1, tokens, rows), lambda i, *_: (i, 0, 0, 0)),
                pl.BlockSpec((2, 1, tokens, columns), lambda i, s, *_: (i, 0, 0, 1 - s[0])),
                pl.BlockSpec(weight.shape, lambda i, *_: (0, 0, 0)),
            ],
            out_specs=[block, block],
            scratch_shapes=[pltpu.SMEM((nodes * capacity,), jnp.int32)],
        ),
        compiler_params=pltpu.CompilerParams(vmem_limit_bytes=VMEM_LIMIT),
        cost_estimate=pl.CostEstimate(
            flops=2 * capacity * tokens * rows * columns,
            bytes_accessed=8 * capacity * rows * columns,
            transcendentals=0,
        ),
    )(side, new_place, new_owner, features, grad_out, weight)


def without(kernel, first, after):
    return lambda *refs: kernel(*refs[:first], *refs[first + len(after) :])


def gradient_kernel(side_ref, features_ref, grad_ref, out_ref):
    out_ref[:, 0] = pair_gradient(out_ref.shape[0], features_ref, grad_ref).astype(jnp.bfloat16)


def gradient_call(nodes, side, features, grad_out, after):
    capacity, _, tokens, rows = features.shape
    columns = grad_out.shape[3] // 2
    pairs = capacity // 2
    shape = (nodes, pairs, 2 * rows // nodes, columns)
    return pl.pallas_call(
        without(gradient_kernel, 3, after),
        out_shape=jax.ShapeDtypeStruct(shape, jnp.bfloat16),
        grid_spec=pltpu.PrefetchScalarGridSpec(
            num_scalar_prefetch=1,
            grid=(pairs,),
            in_specs=[
                pl.BlockSpec((2, 1, tokens, rows), lambda i, s: (i, 0, 0, 0)),
                pl.BlockSpec((2, 1, tokens, columns), lambda i, s: (i, 0, 0, s[0])),
            ]
            + [pl.BlockSpec(memory_space=pl.ANY)] * len(after),
            out_specs=pl.BlockSpec((nodes, 1) + shape[2:], lambda i, s: (0, i, 0, 0)),
        ),
        compiler_params=pltpu.CompilerParams(vmem_limit_bytes=SMALL_LIMIT),
        cost_estimate=pl.CostEstimate(
            flops=2 * capacity * tokens * rows * columns,
            bytes_accessed=4 * capacity * rows * columns,
            transcendentals=0,
        ),
    )(side, features, grad_out, *after)


def arrived_kernel(ahead_ref, out_ref):
    out_ref[...] = jnp.zeros_like(out_ref)


def arrived_call(ahead):
    return pl.pallas_call(
        arrived_kernel,
        out_shape=jax.ShapeDtypeStruct((8, 128), jnp.float32),
        in_specs=[pl.BlockSpec(memory_space=pl.ANY)],
        compiler_params=pltpu.CompilerParams(vmem_limit_bytes=SMALL_LIMIT),
        cost_estimate=pl.CostEstimate(flops=0, bytes_accessed=4096, transcendentals=0),
    )(ahead)


def add_kernel(ours_ref, theirs_ref, out_ref):
    out_ref[...] = (ours_ref[...].astype(jnp.float32) + theirs_ref[...].astype(jnp.float32)).astype(jnp.bfloat16)


def add_call(ours, theirs, after):
    nodes, pairs, pair_rows, columns = ours.shape
    block = pl.BlockSpec((nodes, 1, pair_rows, columns), lambda i: (0, i, 0, 0))
    return pl.pallas_call(
        without(add_kernel, 2, after),
        out_shape=jax.ShapeDtypeStruct(ours.shape, jnp.bfloat16),
        grid=(pairs,),
        in_specs=[block, block] + [pl.BlockSpec(memory_space=pl.ANY)] * len(after),
        out_specs=block,
        compiler_params=pltpu.CompilerParams(vmem_limit_bytes=SMALL_LIMIT),
        cost_estimate=pl.CostEstimate(
            flops=nodes * pairs * pair_rows * columns,
            bytes_accessed=6 * nodes * pairs * pair_rows * columns,
            transcendentals=0,
        ),
    )(ours, theirs, *after)


def update_kernel(place_ref, owner_ref, new_ref, blocks_ref, first_ref, second_ref, send_ref, total, firsts, seconds):
    nodes = send_ref.shape[0]
    experts, rows, width = first_ref.shape
    pair = pl.program_id(0)
    pairs = pl.num_programs(0)

    def block_of(slot):
        position = place_ref[slot]
        both = blocks_ref[position // 2].astype(jnp.float32)
        return jnp.where(position % 2 == 1, both[rows:], both[:rows])

    @pl.when(pair == 0)
    def _():
        @pl.loop(0, experts, unroll=4)
        def _(expert):
            total[expert] = block_of(expert)

        @pl.loop(0, owner_ref.shape[0])
        def _(slot):
            expert = owner_ref[slot]
            total[expert] = total[expert] + block_of(experts + slot)

        @pl.loop(0, experts, unroll=4)
        def _(expert):
            first, second = moments(first_ref[expert], second_ref[expert], total[expert])
            firsts[expert] = first
            seconds[expert] = second

        for array in (firsts, seconds):
            array[experts] = jnp.zeros((rows, width), jnp.float32)

    for node in range(nodes):
        place = (node * pairs + pair) * 2
        left, right = new_ref[place], new_ref[place + 1]
        for which, array in enumerate((firsts, seconds)):
            both = jnp.concatenate([array[left], array[right]], axis=0)
            send_ref[node, which, 0] = both.astype(jnp.bfloat16)


def update_call(blocks, old_place, old_owner, new_table, first, second):
    nodes, pairs, pair_rows, columns = blocks.shape
    experts, rows, _ = first.shape
    whole = pl.BlockSpec(first.shape, lambda i, *_: (0, 0, 0))
    return pl.pallas_call(
        update_kernel,
        out_shape=jax.ShapeDtypeStruct((nodes, 2, pairs, pair_rows, columns), jnp.bfloat16),
        grid_spec=pltpu.PrefetchScalarGridSpec(
            num_scalar_prefetch=3,
            grid=(pairs,),
            in_specs=[
                pl.BlockSpec((nodes * pairs, pair_rows, columns), lambda i, *_: (0, 0, 0)),
                whole,
                whole,
            ],
            out_specs=pl.BlockSpec((nodes, 2, 1, pair_rows, columns), lambda i, *_: (0, 0, i, 0, 0)),
            scratch_shapes=[
                pltpu.VMEM((experts, rows, columns), jnp.float32),
                pltpu.VMEM((experts + 1, rows, columns), jnp.float32),
                pltpu.VMEM((experts + 1, rows, columns), jnp.float32),
            ],
        ),
        compiler_params=pltpu.CompilerParams(vmem_limit_bytes=SMALL_LIMIT),
        cost_estimate=pl.CostEstimate(
            flops=10 * experts * rows * columns,
            bytes_accessed=experts * rows * columns * 8 + 6 * nodes * pairs * pair_rows * columns,
            transcendentals=0,
        ),
    )(old_place, old_owner, new_table, blocks.reshape(nodes * pairs, pair_rows, columns), first, second)


def place_kernel(ahead_ref, got_ref, *out_refs):
    nodes, _, pair_rows, columns = ahead_ref.shape
    rows = pair_rows // 2
    for start in range(0, columns, 128):
        part = slice(start, start + 128)
        first, second = (got_ref[:, which, 0, :, part].astype(jnp.float32) for which in range(2))
        weight = step_weight(ahead_ref[:, 0, :, part].astype(jnp.float32), first, second)
        for out_ref, both in zip(out_refs, (weight, first, second)):
            for side in range(2):
                block = both[:, side * rows : (side + 1) * rows].reshape(nodes * rows, 128)
                out_ref[side, :, part] = block.astype(out_ref.dtype)


def place_call(ahead, got):
    nodes, pairs, pair_rows, columns = ahead.shape
    all_rows = nodes * pair_rows // 2
    return pl.pallas_call(
        place_kernel,
        out_shape=[
            jax.ShapeDtypeStruct((2 * pairs, all_rows, columns), dtype)
            for dtype in (jnp.bfloat16, jnp.float32, jnp.float32)
        ],
        grid=(pairs,),
        in_specs=[
            pl.BlockSpec((nodes, 1, pair_rows, columns), lambda i: (0, i, 0, 0)),
            pl.BlockSpec((nodes, 2, 1, pair_rows, columns), lambda i: (0, 0, i, 0, 0)),
        ],
        out_specs=[pl.BlockSpec((2, all_rows, columns), lambda i: (i, 0, 0))] * 3,
        compiler_params=pltpu.CompilerParams(vmem_limit_bytes=SMALL_LIMIT),
        cost_estimate=pl.CostEstimate(
            flops=20 * nodes * pairs * pair_rows * columns,
            bytes_accessed=16 * nodes * pairs * pair_rows * columns,
            transcendentals=0,
        ),
    )(ahead, got)


def exchange(array):
    return lax.all_to_all(array, "node", split_axis=0, concat_axis=0, tiled=True)


def paired(
    master_weight, first_moment, second_moment, features, grad_out, old_place, new_place, old_owner, new_owner, new_table
):
    nodes = lax.axis_size("node")
    side = jnp.reshape(lax.axis_index("local").astype(jnp.int32), (1,))
    ahead, theirs = front_call(nodes, side, new_place, new_owner, features, grad_out, master_weight)
    ahead = exchange(ahead)
    ours = gradient_call(nodes, side, features, grad_out, (theirs, new_table))
    theirs = lax.ppermute(theirs, "local", [(0, 1), (1, 0)])
    blocks = exchange(add_call(ours, theirs, (arrived_call(ahead),)))
    send = update_call(blocks, old_place, old_owner, new_table, first_moment, second_moment)
    return tuple(place_call(ahead, exchange(send)))


def plain(
    master_weight, first_moment, second_moment, features, grad_out, old_table, new_table
):
    nodes = lax.axis_size("node")
    capacity = features.shape[0]
    experts, rows, columns = master_weight.shape
    slot_grad = jnp.einsum("cltr,cltf->crf", features, grad_out, preferred_element_type=jnp.float32)
    part = lax.psum_scatter(
        slot_grad.astype(jnp.bfloat16), "local", scatter_dimension=2, tiled=True
    )
    part = part.reshape(capacity, nodes, rows, columns).transpose(1, 0, 2, 3)
    blocks = exchange(part).reshape(nodes * capacity, rows, columns).astype(jnp.float32)
    gradient = jnp.zeros((experts + 1, rows, columns), jnp.float32).at[old_table].add(blocks)[:experts]
    got = []
    for array in (master_weight, *moments(first_moment, second_moment, gradient)):
        padded = jnp.concatenate([array.astype(jnp.bfloat16), jnp.zeros((1, rows, columns), jnp.bfloat16)])
        sent = exchange(padded[new_table].reshape(nodes, capacity, rows, columns))
        sent = sent.transpose(1, 0, 2, 3).reshape(capacity, nodes * rows, columns)
        got.append(sent.astype(jnp.float32))
    return step_weight(*got).astype(jnp.bfloat16), got[1], got[2]


def local(
    master_weight,
    first_moment,
    second_moment,
    features,
    grad_out,
    old_place,
    new_place,
    old_owner,
    new_owner,
):
    nodes = lax.axis_size("node")
    capacity = features.shape[0]
    experts, rows, columns = master_weight.shape
    positions = nodes * capacity
    primaries = jnp.arange(experts, dtype=jnp.int32)
    new_table = position_table(new_place, jnp.concatenate([primaries, new_owner]), positions, experts)
    state = (master_weight, first_moment, second_moment, features, grad_out)
    if (
        lax.axis_size("local") == 2
        and capacity % 2 == 0
        and rows % 8 == 0
        and experts % 4 == 0
        and columns % 128 == 0
    ):
        return paired(*state, old_place, new_place, old_owner, new_owner, new_table)
    old_table = position_table(old_place, jnp.concatenate([primaries, old_owner]), positions, experts)
    return plain(*state, old_table, new_table)


def solution(mesh):
    return jax.shard_map(
        local,
        mesh=mesh,
        in_specs=(
            P(None, "node", "local"),
            P(None, "node", "local"),
            P(None, "node", "local"),
            P("node", "local", None, None),
            P("node", "local", None, None),
            P(),
            P(),
            P(),
            P(),
        ),
        out_specs=(P("node", None, "local"), P("node", None, "local"), P("node", None, "local")),
        check_vma=False,
    )
```

```python
import functools

import jax
import jax.numpy as jnp
from jax import lax
from jax.experimental import pallas as pl
from jax.experimental.pallas import tpu as pltpu
from jax.sharding import PartitionSpec as P

BETA_FIRST = 0.9
BETA_SECOND = 0.95
LEARNING_RATE = 0.1
DECAY_RATE = 0.1
EPSILON = 1e-08
CORRECT_FIRST = 1.0 - 0.9**10
CORRECT_SECOND = 1.0 - 0.95**10

VMEM_LIMIT = 64 * 1024 * 1024
SMALL_LIMIT = 28 * 1024 * 1024


def position_table(place, expert, positions, empty):
    match = place[:, None] == jnp.arange(positions, dtype=jnp.int32)[None, :]
    held = jnp.sum(jnp.where(match, expert[:, None] + 1, 0), axis=0)
    return jnp.where(held > 0, held - 1, empty).astype(jnp.int32)


def moments(first_moment, second_moment, gradient):
    first_new = BETA_FIRST * first_moment + (1.0 - BETA_FIRST) * gradient
    second_new = BETA_SECOND * second_moment + (1.0 - BETA_SECOND) * gradient * gradient
    return first_new, second_new


def step_weight(weight_old, first_new, second_new):
    scaled = second_new * (1.0 / CORRECT_SECOND)
    root = scaled * lax.rsqrt(jnp.maximum(scaled, 1e-37))
    update = first_new * (1.0 / CORRECT_FIRST) / (root + EPSILON) + DECAY_RATE * weight_old
    return weight_old - LEARNING_RATE * update


def pair_gradient(nodes, features_ref, grad_ref):
    rows = features_ref.shape[3] // nodes
    parts = []
    for side in range(2):
        product = lax.dot_general(
            features_ref[side, 0],
            grad_ref[side, 0],
            (((0,), (0,)), ((), ())),
            preferred_element_type=jnp.float32,
        )
        parts.append(product.reshape(nodes, rows, product.shape[1]))
    return jnp.concatenate(parts, axis=1)


def front_kernel(side_ref, place_ref, owner_ref, features_ref, grad_ref, weight_ref, ahead_ref, theirs_ref, table):
    nodes = ahead_ref.shape[0]
    experts = weight_ref.shape[0]
    pair = pl.program_id(0)
    pairs = pl.num_programs(0)

    @pl.when(pair == 0)
    def _():
        for position in range(table.shape[0]):
            table[position] = experts
        for expert in range(experts):
            table[place_ref[expert]] = expert
        for slot in range(owner_ref.shape[0]):
            table[place_ref[experts + slot]] = owner_ref[slot]

    theirs_ref[:, 0] = pair_gradient(nodes, features_ref, grad_ref).astype(jnp.bfloat16)
    for node in range(nodes):
        both = []
        for side in range(2):
            expert = table[(node * pairs + pair) * 2 + side]
            held = weight_ref[jnp.minimum(expert, experts - 1)].astype(jnp.float32)
            both.append(jnp.where(expert < experts, held, 0.0))
        ahead_ref[node, 0] = jnp.concatenate(both, axis=0).astype(jnp.bfloat16)


def front_call(nodes, side, new_place, new_owner, features, grad_out, weight):
    capacity, _, tokens, rows = features.shape
    columns = weight.shape[2]
    pairs = capacity // 2
    shape = jax.ShapeDtypeStruct((nodes, pairs, 2 * rows // nodes, columns), jnp.bfloat16)
    block = pl.BlockSpec((nodes, 1) + shape.shape[2:], lambda i, *_: (0, i, 0, 0))
    return pl.pallas_call(
        front_kernel,
        out_shape=[shape, shape],
        grid_spec=pltpu.PrefetchScalarGridSpec(
            num_scalar_prefetch=3,
            grid=(pairs,),
            in_specs=[
                pl.BlockSpec((2, 1, tokens, rows), lambda i, *_: (i, 0, 0, 0)),
                pl.BlockSpec((2, 1, tokens, columns), lambda i, s, *_: (i, 0, 0, 1 - s[0])),
                pl.BlockSpec(weight.shape, lambda i, *_: (0, 0, 0)),
            ],
            out_specs=[block, block],
            scratch_shapes=[pltpu.SMEM((nodes * capacity,), jnp.int32)],
        ),
        compiler_params=pltpu.CompilerParams(vmem_limit_bytes=VMEM_LIMIT),
        cost_estimate=pl.CostEstimate(
            flops=2 * capacity * tokens * rows * columns,
            bytes_accessed=8 * capacity * rows * columns,
            transcendentals=0,
        ),
    )(side, new_place, new_owner, features, grad_out, weight)


def without(kernel, first, after):
    return lambda *refs: kernel(*refs[:first], *refs[first + len(after) :])


def gradient_kernel(side_ref, features_ref, grad_ref, out_ref):
    out_ref[:, 0] = pair_gradient(out_ref.shape[0], features_ref, grad_ref).astype(jnp.bfloat16)


def gradient_call(nodes, side, features, grad_out, after):
    capacity, _, tokens, rows = features.shape
    columns = grad_out.shape[3] // 2
    pairs = capacity // 2
    shape = (nodes, pairs, 2 * rows // nodes, columns)
    return pl.pallas_call(
        without(gradient_kernel, 3, after),
        out_shape=jax.ShapeDtypeStruct(shape, jnp.bfloat16),
        grid_spec=pltpu.PrefetchScalarGridSpec(
            num_scalar_prefetch=1,
            grid=(pairs,),
            in_specs=[
                pl.BlockSpec((2, 1, tokens, rows), lambda i, s: (i, 0, 0, 0)),
                pl.BlockSpec((2, 1, tokens, columns), lambda i, s: (i, 0, 0, s[0])),
            ]
            + [pl.BlockSpec(memory_space=pl.ANY)] * len(after),
            out_specs=pl.BlockSpec((nodes, 1) + shape[2:], lambda i, s: (0, i, 0, 0)),
        ),
        compiler_params=pltpu.CompilerParams(vmem_limit_bytes=SMALL_LIMIT),
        cost_estimate=pl.CostEstimate(
            flops=2 * capacity * tokens * rows * columns,
            bytes_accessed=4 * capacity * rows * columns,
            transcendentals=0,
        ),
    )(side, features, grad_out, *after)


def arrived_kernel(ahead_ref, out_ref):
    out_ref[...] = jnp.zeros_like(out_ref)


def arrived_call(ahead):
    return pl.pallas_call(
        arrived_kernel,
        out_shape=jax.ShapeDtypeStruct((8, 128), jnp.float32),
        in_specs=[pl.BlockSpec(memory_space=pl.ANY)],
        compiler_params=pltpu.CompilerParams(vmem_limit_bytes=SMALL_LIMIT),
        cost_estimate=pl.CostEstimate(flops=0, bytes_accessed=4096, transcendentals=0),
    )(ahead)


def add_kernel(ours_ref, theirs_ref, out_ref):
    out_ref[...] = (ours_ref[...].astype(jnp.float32) + theirs_ref[...].astype(jnp.float32)).astype(jnp.bfloat16)


def add_call(ours, theirs, after):
    nodes, pairs, pair_rows, columns = ours.shape
    block = pl.BlockSpec((nodes, 1, pair_rows, columns), lambda i: (0, i, 0, 0))
    return pl.pallas_call(
        without(add_kernel, 2, after),
        out_shape=jax.ShapeDtypeStruct(ours.shape, jnp.bfloat16),
        grid=(pairs,),
        in_specs=[block, block] + [pl.BlockSpec(memory_space=pl.ANY)] * len(after),
        out_specs=block,
        compiler_params=pltpu.CompilerParams(vmem_limit_bytes=SMALL_LIMIT),
        cost_estimate=pl.CostEstimate(
            flops=nodes * pairs * pair_rows * columns,
            bytes_accessed=6 * nodes * pairs * pair_rows * columns,
            transcendentals=0,
        ),
    )(ours, theirs, *after)


def update_kernel(place_ref, owner_ref, new_ref, blocks_ref, first_ref, second_ref, send_ref, total, firsts, seconds):
    nodes = send_ref.shape[0]
    experts, rows, width = first_ref.shape
    pair = pl.program_id(0)
    pairs = pl.num_programs(0)

    def block_of(slot):
        position = place_ref[slot]
        both = blocks_ref[position // 2].astype(jnp.float32)
        return jnp.where(position % 2 == 1, both[rows:], both[:rows])

    @pl.when(pair == 0)
    def _():
        @pl.loop(0, experts, unroll=4)
        def _(expert):
            total[expert] = block_of(expert)

        @pl.loop(0, owner_ref.shape[0])
        def _(slot):
            expert = owner_ref[slot]
            total[expert] = total[expert] + block_of(experts + slot)

        @pl.loop(0, experts, unroll=4)
        def _(expert):
            first, second = moments(first_ref[expert], second_ref[expert], total[expert])
            firsts[expert] = first
            seconds[expert] = second

        for array in (firsts, seconds):
            array[experts] = jnp.zeros((rows, width), jnp.float32)

    for node in range(nodes):
        place = (node * pairs + pair) * 2
        left, right = new_ref[place], new_ref[place + 1]
        for which, array in enumerate((firsts, seconds)):
            both = jnp.concatenate([array[left], array[right]], axis=0)
            send_ref[node, which, 0] = both.astype(jnp.bfloat16)


def update_call(blocks, old_place, old_owner, new_table, first, second):
    nodes, pairs, pair_rows, columns = blocks.shape
    experts, rows, _ = first.shape
    whole = pl.BlockSpec(first.shape, lambda i, *_: (0, 0, 0))
    return pl.pallas_call(
        update_kernel,
        out_shape=jax.ShapeDtypeStruct((nodes, 2, pairs, pair_rows, columns), jnp.bfloat16),
        grid_spec=pltpu.PrefetchScalarGridSpec(
            num_scalar_prefetch=3,
            grid=(pairs,),
            in_specs=[
                pl.BlockSpec((nodes * pairs, pair_rows, columns), lambda i, *_: (0, 0, 0)),
                whole,
                whole,
            ],
            out_specs=pl.BlockSpec((nodes, 2, 1, pair_rows, columns), lambda i, *_: (0, 0, i, 0, 0)),
            scratch_shapes=[
                pltpu.VMEM((experts, rows, columns), jnp.float32),
                pltpu.VMEM((experts + 1, rows, columns), jnp.float32),
                pltpu.VMEM((experts + 1, rows, columns), jnp.float32),
            ],
        ),
        compiler_params=pltpu.CompilerParams(vmem_limit_bytes=SMALL_LIMIT),
        cost_estimate=pl.CostEstimate(
            flops=10 * experts * rows * columns,
            bytes_accessed=experts * rows * columns * 8 + 6 * nodes * pairs * pair_rows * columns,
            transcendentals=0,
        ),
    )(old_place, old_owner, new_table, blocks.reshape(nodes * pairs, pair_rows, columns), first, second)


def place_kernel(ahead_ref, got_ref, *out_refs):
    nodes, _, pair_rows, columns = ahead_ref.shape
    rows = pair_rows // 2
    for start in range(0, columns, 128):
        part = slice(start, start + 128)
        first, second = (got_ref[:, which, 0, :, part].astype(jnp.float32) for which in range(2))
        weight = step_weight(ahead_ref[:, 0, :, part].astype(jnp.float32), first, second)
        for out_ref, both in zip(out_refs, (weight, first, second)):
            for side in range(2):
                block = both[:, side * rows : (side + 1) * rows].reshape(nodes * rows, 128)
                out_ref[side, :, part] = block.astype(out_ref.dtype)


def place_call(ahead, got):
    nodes, pairs, pair_rows, columns = ahead.shape
    all_rows = nodes * pair_rows // 2
    return pl.pallas_call(
        place_kernel,
        out_shape=[
            jax.ShapeDtypeStruct((2 * pairs, all_rows, columns), dtype)
            for dtype in (jnp.bfloat16, jnp.float32, jnp.float32)
        ],
        grid=(pairs,),
        in_specs=[
            pl.BlockSpec((nodes, 1, pair_rows, columns), lambda i: (0, i, 0, 0)),
            pl.BlockSpec((nodes, 2, 1, pair_rows, columns), lambda i: (0, 0, i, 0, 0)),
        ],
        out_specs=[pl.BlockSpec((2, all_rows, columns), lambda i: (i, 0, 0))] * 3,
        compiler_params=pltpu.CompilerParams(vmem_limit_bytes=SMALL_LIMIT),
        cost_estimate=pl.CostEstimate(
            flops=20 * nodes * pairs * pair_rows * columns,
            bytes_accessed=16 * nodes * pairs * pair_rows * columns,
            transcendentals=0,
        ),
    )(ahead, got)


def exchange(array):
    return lax.all_to_all(array, "node", split_axis=0, concat_axis=0, tiled=True)


def paired(
    master_weight, first_moment, second_moment, features, grad_out, old_place, new_place, old_owner, new_owner, new_table
):
    nodes = lax.axis_size("node")
    side = jnp.reshape(lax.axis_index("local").astype(jnp.int32), (1,))
    ahead, theirs = front_call(nodes, side, new_place, new_owner, features, grad_out, master_weight)
    ahead = exchange(ahead)
    ours = gradient_call(nodes, side, features, grad_out, (theirs, new_table))
    theirs = lax.ppermute(theirs, "local", [(0, 1), (1, 0)])
    blocks = exchange(add_call(ours, theirs, (arrived_call(ahead),)))
    send = update_call(blocks, old_place, old_owner, new_table, first_moment, second_moment)
    return tuple(place_call(ahead, exchange(send)))


def plain(
    master_weight, first_moment, second_moment, features, grad_out, old_table, new_table
):
    nodes = lax.axis_size("node")
    capacity = features.shape[0]
    experts, rows, columns = master_weight.shape
    slot_grad = jnp.einsum("cltr,cltf->crf", features, grad_out, preferred_element_type=jnp.float32)
    part = lax.psum_scatter(
        slot_grad.astype(jnp.bfloat16), "local", scatter_dimension=2, tiled=True
    )
    part = part.reshape(capacity, nodes, rows, columns).transpose(1, 0, 2, 3)
    blocks = exchange(part).reshape(nodes * capacity, rows, columns).astype(jnp.float32)
    gradient = jnp.zeros((experts + 1, rows, columns), jnp.float32).at[old_table].add(blocks)[:experts]
    got = []
    for array in (master_weight, *moments(first_moment, second_moment, gradient)):
        padded = jnp.concatenate([array.astype(jnp.bfloat16), jnp.zeros((1, rows, columns), jnp.bfloat16)])
        sent = exchange(padded[new_table].reshape(nodes, capacity, rows, columns))
        sent = sent.transpose(1, 0, 2, 3).reshape(capacity, nodes * rows, columns)
        got.append(sent.astype(jnp.float32))
    return step_weight(*got).astype(jnp.bfloat16), got[1], got[2]


def local(
    master_weight,
    first_moment,
    second_moment,
    features,
    grad_out,
    old_place,
    new_place,
    old_owner,
    new_owner,
):
    nodes = lax.axis_size("node")
    capacity = features.shape[0]
    experts, rows, columns = master_weight.shape
    positions = nodes * capacity
    primaries = jnp.arange(experts, dtype=jnp.int32)
    new_table = position_table(new_place, jnp.concatenate([primaries, new_owner]), positions, experts)
    state = (master_weight, first_moment, second_moment, features, grad_out)
    if (
        lax.axis_size("local") == 2
        and capacity % 2 == 0
        and rows % 8 == 0
        and experts % 4 == 0
        and columns % 128 == 0
    ):
        return paired(*state, old_place, new_place, old_owner, new_owner, new_table)
    old_table = position_table(old_place, jnp.concatenate([primaries, old_owner]), positions, experts)
    return plain(*state, old_table, new_table)


def solution(mesh):
    return jax.shard_map(
        local,
        mesh=mesh,
        in_specs=(
            P(None, "node", "local"),
            P(None, "node", "local"),
            P(None, "node", "local"),
            P("node", "local", None, None),
            P("node", "local", None, None),
            P(),
            P(),
            P(),
            P(),
        ),
        out_specs=(P("node", None, "local"), P("node", None, "local"), P("node", None, "local")),
        check_vma=False,
    )
```

```python
import functools

import jax
import jax.numpy as jnp
from jax import lax
from jax.experimental import pallas as pl
from jax.experimental.pallas import tpu as pltpu
from jax.sharding import PartitionSpec as P

BETA_FIRST = 0.9
BETA_SECOND = 0.95
LEARNING_RATE = 0.1
DECAY_RATE = 0.1
EPSILON = 1e-08
CORRECT_FIRST = 1.0 - 0.9**10
CORRECT_SECOND = 1.0 - 0.95**10

VMEM_LIMIT = 64 * 1024 * 1024
SMALL_LIMIT = 28 * 1024 * 1024


def position_table(place, expert, positions, empty):
    match = place[:, None] == jnp.arange(positions, dtype=jnp.int32)[None, :]
    held = jnp.sum(jnp.where(match, expert[:, None] + 1, 0), axis=0)
    return jnp.where(held > 0, held - 1, empty).astype(jnp.int32)


def moments(first_moment, second_moment, gradient):
    first_new = BETA_FIRST * first_moment + (1.0 - BETA_FIRST) * gradient
    second_new = BETA_SECOND * second_moment + (1.0 - BETA_SECOND) * gradient * gradient
    return first_new, second_new


def step_weight(weight_old, first_new, second_new):
    scaled = second_new * (1.0 / CORRECT_SECOND)
    root = scaled * lax.rsqrt(jnp.maximum(scaled, 1e-37))
    update = first_new * (1.0 / CORRECT_FIRST) / (root + EPSILON) + DECAY_RATE * weight_old
    return weight_old - LEARNING_RATE * update


def pair_gradient(nodes, features_ref, grad_ref):
    rows = features_ref.shape[3] // nodes
    parts = []
    for side in range(2):
        product = lax.dot_general(
            features_ref[side, 0],
            grad_ref[side, 0],
            (((0,), (0,)), ((), ())),
            preferred_element_type=jnp.float32,
        )
        parts.append(product.reshape(nodes, rows, product.shape[1]))
    return jnp.concatenate(parts, axis=1)


def front_kernel(side_ref, place_ref, owner_ref, features_ref, grad_ref, weight_ref, ahead_ref, low_ref, high_ref, table):
    nodes = ahead_ref.shape[0]
    experts = weight_ref.shape[0]
    pair = pl.program_id(0)
    pairs = pl.num_programs(0)

    @pl.when(pair == 0)
    def _():
        for position in range(table.shape[0]):
            table[position] = experts
        for expert in range(experts):
            table[place_ref[expert]] = expert
        for slot in range(owner_ref.shape[0]):
            table[place_ref[experts + slot]] = owner_ref[slot]

    theirs = pair_gradient(nodes, features_ref, grad_ref).astype(jnp.bfloat16)
    width = low_ref.shape[3]
    low_ref[:, 0] = theirs[:, :, :width]
    high_ref[:, 0] = theirs[:, :, width:]
    for node in range(nodes):
        both = []
        for side in range(2):
            expert = table[(node * pairs + pair) * 2 + side]
            held = weight_ref[jnp.minimum(expert, experts - 1)].astype(jnp.float32)
            both.append(jnp.where(expert < experts, held, 0.0))
        ahead_ref[node, 0] = jnp.concatenate(both, axis=0).astype(jnp.bfloat16)


def front_call(nodes, side, new_place, new_owner, features, grad_out, weight):
    capacity, _, tokens, rows = features.shape
    columns = weight.shape[2]
    pairs = capacity // 2
    shape = jax.ShapeDtypeStruct((nodes, pairs, 2 * rows // nodes, columns), jnp.bfloat16)
    block = pl.BlockSpec((nodes, 1) + shape.shape[2:], lambda i, *_: (0, i, 0, 0))
    part = jax.ShapeDtypeStruct(shape.shape[:3] + (columns // 2,), jnp.bfloat16)
    part_block = pl.BlockSpec((nodes, 1) + part.shape[2:], lambda i, *_: (0, i, 0, 0))
    return pl.pallas_call(
        front_kernel,
        out_shape=[shape, part, part],
        grid_spec=pltpu.PrefetchScalarGridSpec(
            num_scalar_prefetch=3,
            grid=(pairs,),
            in_specs=[
                pl.BlockSpec((2, 1, tokens, rows), lambda i, *_: (i, 0, 0, 0)),
                pl.BlockSpec((2, 1, tokens, columns), lambda i, s, *_: (i, 0, 0, 1 - s[0])),
                pl.BlockSpec(weight.shape, lambda i, *_: (0, 0, 0)),
            ],
            out_specs=[block, part_block, part_block],
            scratch_shapes=[pltpu.SMEM((nodes * capacity,), jnp.int32)],
        ),
        compiler_params=pltpu.CompilerParams(vmem_limit_bytes=VMEM_LIMIT),
        cost_estimate=pl.CostEstimate(
            flops=2 * capacity * tokens * rows * columns,
            bytes_accessed=8 * capacity * rows * columns,
            transcendentals=0,
        ),
    )(side, new_place, new_owner, features, grad_out, weight)


def without(kernel, first, after):
    return lambda *refs: kernel(*refs[:first], *refs[first + len(after) :])


def gradient_kernel(side_ref, features_ref, grad_ref, out_ref):
    out_ref[:, 0] = pair_gradient(out_ref.shape[0], features_ref, grad_ref).astype(jnp.bfloat16)


def gradient_call(nodes, side, features, grad_out, after):
    capacity, _, tokens, rows = features.shape
    columns = grad_out.shape[3] // 2
    pairs = capacity // 2
    shape = (nodes, pairs, 2 * rows // nodes, columns)
    return pl.pallas_call(
        without(gradient_kernel, 3, after),
        out_shape=jax.ShapeDtypeStruct(shape, jnp.bfloat16),
        grid_spec=pltpu.PrefetchScalarGridSpec(
            num_scalar_prefetch=1,
            grid=(pairs,),
            in_specs=[
                pl.BlockSpec((2, 1, tokens, rows), lambda i, s: (i, 0, 0, 0)),
                pl.BlockSpec((2, 1, tokens, columns), lambda i, s: (i, 0, 0, s[0])),
            ]
            + [pl.BlockSpec(memory_space=pl.ANY)] * len(after),
            out_specs=pl.BlockSpec((nodes, 1) + shape[2:], lambda i, s: (0, i, 0, 0)),
        ),
        compiler_params=pltpu.CompilerParams(vmem_limit_bytes=SMALL_LIMIT),
        cost_estimate=pl.CostEstimate(
            flops=2 * capacity * tokens * rows * columns,
            bytes_accessed=4 * capacity * rows * columns,
            transcendentals=0,
        ),
    )(side, features, grad_out, *after)


def arrived_kernel(ahead_ref, out_ref):
    out_ref[...] = jnp.zeros_like(out_ref)


def arrived_call(ahead):
    return pl.pallas_call(
        arrived_kernel,
        out_shape=jax.ShapeDtypeStruct((8, 128), jnp.float32),
        in_specs=[pl.BlockSpec(memory_space=pl.ANY)],
        compiler_params=pltpu.CompilerParams(vmem_limit_bytes=SMALL_LIMIT),
        cost_estimate=pl.CostEstimate(flops=0, bytes_accessed=4096, transcendentals=0),
    )(ahead)


def add_kernel(ours_ref, theirs_ref, out_ref):
    out_ref[...] = (ours_ref[...].astype(jnp.float32) + theirs_ref[...].astype(jnp.float32)).astype(jnp.bfloat16)


def add_call(which, ours, theirs, before=(), after=()):
    nodes, pairs, pair_rows, width = theirs.shape
    block = pl.BlockSpec((nodes, 1, pair_rows, width), lambda i: (0, i, 0, 0))
    side = pl.BlockSpec((nodes, 1, pair_rows, width), lambda i: (0, i, 0, which))
    unread = (*before, *after)
    return pl.pallas_call(
        without(add_kernel, 2, unread),
        out_shape=jax.ShapeDtypeStruct(ours.shape, jnp.bfloat16),
        grid=(pairs,),
        in_specs=[side, block] + [pl.BlockSpec(memory_space=pl.ANY)] * len(unread),
        out_specs=side,
        input_output_aliases={2: 0} if before else {},
        compiler_params=pltpu.CompilerParams(vmem_limit_bytes=SMALL_LIMIT),
        cost_estimate=pl.CostEstimate(
            flops=nodes * pairs * pair_rows * width,
            bytes_accessed=6 * nodes * pairs * pair_rows * width,
            transcendentals=0,
        ),
    )(ours, theirs, *unread)


def update_kernel(place_ref, owner_ref, new_ref, blocks_ref, first_ref, second_ref, send_ref, total, firsts, seconds):
    nodes = send_ref.shape[0]
    experts, rows, width = first_ref.shape
    pair = pl.program_id(0)
    pairs = pl.num_programs(0)

    def block_of(slot):
        position = place_ref[slot]
        both = blocks_ref[position // 2].astype(jnp.float32)
        return jnp.where(position % 2 == 1, both[rows:], both[:rows])

    @pl.when(pair == 0)
    def _():
        @pl.loop(0, experts, unroll=4)
        def _(expert):
            total[expert] = block_of(expert)

        @pl.loop(0, owner_ref.shape[0])
        def _(slot):
            expert = owner_ref[slot]
            total[expert] = total[expert] + block_of(experts + slot)

        @pl.loop(0, experts, unroll=4)
        def _(expert):
            first, second = moments(first_ref[expert], second_ref[expert], total[expert])
            firsts[expert] = first
            seconds[expert] = second

        for array in (firsts, seconds):
            array[experts] = jnp.zeros((rows, width), jnp.float32)

    for node in range(nodes):
        place = (node * pairs + pair) * 2
        left, right = new_ref[place], new_ref[place + 1]
        for which, array in enumerate((firsts, seconds)):
            both = jnp.concatenate([array[left], array[right]], axis=0)
            send_ref[node, which, 0] = both.astype(jnp.bfloat16)


def update_call(blocks, old_place, old_owner, new_table, first, second):
    nodes, pairs, pair_rows, columns = blocks.shape
    experts, rows, _ = first.shape
    whole = pl.BlockSpec(first.shape, lambda i, *_: (0, 0, 0))
    return pl.pallas_call(
        update_kernel,
        out_shape=jax.ShapeDtypeStruct((nodes, 2, pairs, pair_rows, columns), jnp.bfloat16),
        grid_spec=pltpu.PrefetchScalarGridSpec(
            num_scalar_prefetch=3,
            grid=(pairs,),
            in_specs=[
                pl.BlockSpec((nodes * pairs, pair_rows, columns), lambda i, *_: (0, 0, 0)),
                whole,
                whole,
            ],
            out_specs=pl.BlockSpec((nodes, 2, 1, pair_rows, columns), lambda i, *_: (0, 0, i, 0, 0)),
            scratch_shapes=[
                pltpu.VMEM((experts, rows, columns), jnp.float32),
                pltpu.VMEM((experts + 1, rows, columns), jnp.float32),
                pltpu.VMEM((experts + 1, rows, columns), jnp.float32),
            ],
        ),
        compiler_params=pltpu.CompilerParams(vmem_limit_bytes=SMALL_LIMIT),
        cost_estimate=pl.CostEstimate(
            flops=10 * experts * rows * columns,
            bytes_accessed=experts * rows * columns * 8 + 6 * nodes * pairs * pair_rows * columns,
            transcendentals=0,
        ),
    )(old_place, old_owner, new_table, blocks.reshape(nodes * pairs, pair_rows, columns), first, second)


def place_kernel(ahead_ref, got_ref, *out_refs):
    nodes, _, pair_rows, columns = ahead_ref.shape
    rows = pair_rows // 2
    for start in range(0, columns, 128):
        part = slice(start, start + 128)
        first, second = (got_ref[:, which, 0, :, part].astype(jnp.float32) for which in range(2))
        weight = step_weight(ahead_ref[:, 0, :, part].astype(jnp.float32), first, second)
        for out_ref, both in zip(out_refs, (weight, first, second)):
            for side in range(2):
                block = both[:, side * rows : (side + 1) * rows].reshape(nodes * rows, 128)
                out_ref[side, :, part] = block.astype(out_ref.dtype)


def place_call(ahead, got):
    nodes, pairs, pair_rows, columns = ahead.shape
    all_rows = nodes * pair_rows // 2
    return pl.pallas_call(
        place_kernel,
        out_shape=[
            jax.ShapeDtypeStruct((2 * pairs, all_rows, columns), dtype)
            for dtype in (jnp.bfloat16, jnp.float32, jnp.float32)
        ],
        grid=(pairs,),
        in_specs=[
            pl.BlockSpec((nodes, 1, pair_rows, columns), lambda i: (0, i, 0, 0)),
            pl.BlockSpec((nodes, 2, 1, pair_rows, columns), lambda i: (0, 0, i, 0, 0)),
        ],
        out_specs=[pl.BlockSpec((2, all_rows, columns), lambda i: (i, 0, 0))] * 3,
        compiler_params=pltpu.CompilerParams(vmem_limit_bytes=SMALL_LIMIT),
        cost_estimate=pl.CostEstimate(
            flops=20 * nodes * pairs * pair_rows * columns,
            bytes_accessed=16 * nodes * pairs * pair_rows * columns,
            transcendentals=0,
        ),
    )(ahead, got)


def exchange(array):
    return lax.all_to_all(array, "node", split_axis=0, concat_axis=0, tiled=True)


def paired(
    master_weight, first_moment, second_moment, features, grad_out, old_place, new_place, old_owner, new_owner, new_table
):
    nodes = lax.axis_size("node")
    side = jnp.reshape(lax.axis_index("local").astype(jnp.int32), (1,))
    ahead, *theirs = front_call(nodes, side, new_place, new_owner, features, grad_out, master_weight)
    ahead = exchange(ahead)
    ours = gradient_call(nodes, side, features, grad_out, (*theirs, new_table))
    low, high = (lax.ppermute(part, "local", [(0, 1), (1, 0)]) for part in theirs)
    blocks = add_call(0, ours, low)
    blocks = exchange(add_call(1, ours, high, (blocks,), (arrived_call(ahead),)))
    send = update_call(blocks, old_place, old_owner, new_table, first_moment, second_moment)
    return tuple(place_call(ahead, exchange(send)))


def plain(
    master_weight, first_moment, second_moment, features, grad_out, old_table, new_table
):
    nodes = lax.axis_size("node")
    capacity = features.shape[0]
    experts, rows, columns = master_weight.shape
    slot_grad = jnp.einsum("cltr,cltf->crf", features, grad_out, preferred_element_type=jnp.float32)
    part = lax.psum_scatter(
        slot_grad.astype(jnp.bfloat16), "local", scatter_dimension=2, tiled=True
    )
    part = part.reshape(capacity, nodes, rows, columns).transpose(1, 0, 2, 3)
    blocks = exchange(part).reshape(nodes * capacity, rows, columns).astype(jnp.float32)
    gradient = jnp.zeros((experts + 1, rows, columns), jnp.float32).at[old_table].add(blocks)[:experts]
    got = []
    for array in (master_weight, *moments(first_moment, second_moment, gradient)):
        padded = jnp.concatenate([array.astype(jnp.bfloat16), jnp.zeros((1, rows, columns), jnp.bfloat16)])
        sent = exchange(padded[new_table].reshape(nodes, capacity, rows, columns))
        sent = sent.transpose(1, 0, 2, 3).reshape(capacity, nodes * rows, columns)
        got.append(sent.astype(jnp.float32))
    return step_weight(*got).astype(jnp.bfloat16), got[1], got[2]


def local(
    master_weight,
    first_moment,
    second_moment,
    features,
    grad_out,
    old_place,
    new_place,
    old_owner,
    new_owner,
):
    nodes = lax.axis_size("node")
    capacity = features.shape[0]
    experts, rows, columns = master_weight.shape
    positions = nodes * capacity
    primaries = jnp.arange(experts, dtype=jnp.int32)
    new_table = position_table(new_place, jnp.concatenate([primaries, new_owner]), positions, experts)
    state = (master_weight, first_moment, second_moment, features, grad_out)
    if (
        lax.axis_size("local") == 2
        and capacity % 2 == 0
        and rows % 8 == 0
        and experts % 4 == 0
        and columns % 256 == 0
    ):
        return paired(*state, old_place, new_place, old_owner, new_owner, new_table)
    old_table = position_table(old_place, jnp.concatenate([primaries, old_owner]), positions, experts)
    return plain(*state, old_table, new_table)


def solution(mesh):
    return jax.shard_map(
        local,
        mesh=mesh,
        in_specs=(
            P(None, "node", "local"),
            P(None, "node", "local"),
            P(None, "node", "local"),
            P("node", "local", None, None),
            P("node", "local", None, None),
            P(),
            P(),
            P(),
            P(),
        ),
        out_specs=(P("node", None, "local"), P("node", None, "local"), P("node", None, "local")),
        check_vma=False,
    )
```

```python
import functools

import jax
import jax.numpy as jnp
from jax import lax
from jax.experimental import pallas as pl
from jax.experimental.pallas import tpu as pltpu
from jax.sharding import PartitionSpec as P

BETA_FIRST = 0.9
BETA_SECOND = 0.95
LEARNING_RATE = 0.1
DECAY_RATE = 0.1
EPSILON = 1e-08
CORRECT_FIRST = 1.0 - 0.9**10
CORRECT_SECOND = 1.0 - 0.95**10

VMEM_LIMIT = 64 * 1024 * 1024
SMALL_LIMIT = 28 * 1024 * 1024


def position_table(place, expert, positions, empty):
    match = place[:, None] == jnp.arange(positions, dtype=jnp.int32)[None, :]
    held = jnp.sum(jnp.where(match, expert[:, None] + 1, 0), axis=0)
    return jnp.where(held > 0, held - 1, empty).astype(jnp.int32)


def moments(first_moment, second_moment, gradient):
    first_new = BETA_FIRST * first_moment + (1.0 - BETA_FIRST) * gradient
    second_new = BETA_SECOND * second_moment + (1.0 - BETA_SECOND) * gradient * gradient
    return first_new, second_new


def step_weight(weight_old, first_new, second_new):
    scaled = second_new * (1.0 / CORRECT_SECOND)
    root = scaled * lax.rsqrt(jnp.maximum(scaled, 1e-37))
    update = first_new * (1.0 / CORRECT_FIRST) / (root + EPSILON) + DECAY_RATE * weight_old
    return weight_old - LEARNING_RATE * update


def pair_gradient(nodes, features_ref, grad_ref):
    rows = features_ref.shape[3] // nodes
    parts = []
    for side in range(2):
        product = lax.dot_general(
            features_ref[side, 0],
            grad_ref[side, 0],
            (((0,), (0,)), ((), ())),
            preferred_element_type=jnp.float32,
        )
        parts.append(product.reshape(nodes, rows, product.shape[1]))
    return jnp.concatenate(parts, axis=1)


def front_kernel(side_ref, place_ref, owner_ref, features_ref, grad_ref, weight_ref, ahead_ref, low_ref, high_ref, table):
    nodes = ahead_ref.shape[0]
    experts = weight_ref.shape[0]
    pair = pl.program_id(0)
    pairs = pl.num_programs(0)

    @pl.when(pair == 0)
    def _():
        for position in range(table.shape[0]):
            table[position] = experts
        for expert in range(experts):
            table[place_ref[expert]] = expert
        for slot in range(owner_ref.shape[0]):
            table[place_ref[experts + slot]] = owner_ref[slot]

    theirs = pair_gradient(nodes, features_ref, grad_ref).astype(jnp.bfloat16)
    width = low_ref.shape[3]
    low_ref[:, 0] = theirs[:, :, :width]
    high_ref[:, 0] = theirs[:, :, width:]
    for node in range(nodes):
        both = []
        for side in range(2):
            expert = table[(node * pairs + pair) * 2 + side]
            held = weight_ref[jnp.minimum(expert, experts - 1)].astype(jnp.float32)
            both.append(jnp.where(expert < experts, held, 0.0))
        ahead_ref[node, 0] = jnp.concatenate(both, axis=0).astype(jnp.bfloat16)


def front_call(nodes, side, new_place, new_owner, features, grad_out, weight):
    capacity, _, tokens, rows = features.shape
    columns = weight.shape[2]
    pairs = capacity // 2
    shape = jax.ShapeDtypeStruct((nodes, pairs, 2 * rows // nodes, columns), jnp.bfloat16)
    block = pl.BlockSpec((nodes, 1) + shape.shape[2:], lambda i, *_: (0, i, 0, 0))
    widths = (columns * 7 // 8, columns // 8)
    parts = [jax.ShapeDtypeStruct(shape.shape[:3] + (width,), jnp.bfloat16) for width in widths]
    part_blocks = [pl.BlockSpec((nodes, 1) + part.shape[2:], lambda i, *_: (0, i, 0, 0)) for part in parts]
    return pl.pallas_call(
        front_kernel,
        out_shape=[shape, *parts],
        grid_spec=pltpu.PrefetchScalarGridSpec(
            num_scalar_prefetch=3,
            grid=(pairs,),
            in_specs=[
                pl.BlockSpec((2, 1, tokens, rows), lambda i, *_: (i, 0, 0, 0)),
                pl.BlockSpec((2, 1, tokens, columns), lambda i, s, *_: (i, 0, 0, 1 - s[0])),
                pl.BlockSpec(weight.shape, lambda i, *_: (0, 0, 0)),
            ],
            out_specs=[block, *part_blocks],
            scratch_shapes=[pltpu.SMEM((nodes * capacity,), jnp.int32)],
        ),
        compiler_params=pltpu.CompilerParams(vmem_limit_bytes=VMEM_LIMIT),
        cost_estimate=pl.CostEstimate(
            flops=2 * capacity * tokens * rows * columns,
            bytes_accessed=8 * capacity * rows * columns,
            transcendentals=0,
        ),
    )(side, new_place, new_owner, features, grad_out, weight)


def without(kernel, first, after):
    return lambda *refs: kernel(*refs[:first], *refs[first + len(after) :])


def gradient_kernel(side_ref, features_ref, grad_ref, out_ref):
    out_ref[:, 0] = pair_gradient(out_ref.shape[0], features_ref, grad_ref).astype(jnp.bfloat16)


def gradient_call(nodes, side, features, grad_out, after):
    capacity, _, tokens, rows = features.shape
    columns = grad_out.shape[3] // 2
    pairs = capacity // 2
    shape = (nodes, pairs, 2 * rows // nodes, columns)
    return pl.pallas_call(
        without(gradient_kernel, 3, after),
        out_shape=jax.ShapeDtypeStruct(shape, jnp.bfloat16),
        grid_spec=pltpu.PrefetchScalarGridSpec(
            num_scalar_prefetch=1,
            grid=(pairs,),
            in_specs=[
                pl.BlockSpec((2, 1, tokens, rows), lambda i, s: (i, 0, 0, 0)),
                pl.BlockSpec((2, 1, tokens, columns), lambda i, s: (i, 0, 0, s[0])),
            ]
            + [pl.BlockSpec(memory_space=pl.ANY)] * len(after),
            out_specs=pl.BlockSpec((nodes, 1) + shape[2:], lambda i, s: (0, i, 0, 0)),
        ),
        compiler_params=pltpu.CompilerParams(vmem_limit_bytes=SMALL_LIMIT),
        cost_estimate=pl.CostEstimate(
            flops=2 * capacity * tokens * rows * columns,
            bytes_accessed=4 * capacity * rows * columns,
            transcendentals=0,
        ),
    )(side, features, grad_out, *after)


def arrived_kernel(ahead_ref, out_ref):
    out_ref[...] = jnp.zeros_like(out_ref)


def arrived_call(ahead):
    return pl.pallas_call(
        arrived_kernel,
        out_shape=jax.ShapeDtypeStruct((8, 128), jnp.float32),
        in_specs=[pl.BlockSpec(memory_space=pl.ANY)],
        compiler_params=pltpu.CompilerParams(vmem_limit_bytes=SMALL_LIMIT),
        cost_estimate=pl.CostEstimate(flops=0, bytes_accessed=4096, transcendentals=0),
    )(ahead)


def add_kernel(ours_ref, theirs_ref, out_ref):
    out_ref[...] = (ours_ref[...].astype(jnp.float32) + theirs_ref[...].astype(jnp.float32)).astype(jnp.bfloat16)


def add_call(which, ours, theirs, before=(), after=()):
    nodes, pairs, pair_rows, width = theirs.shape
    block = pl.BlockSpec((nodes, 1, pair_rows, width), lambda i: (0, i, 0, 0))
    side = pl.BlockSpec((nodes, 1, pair_rows, width), lambda i: (0, i, 0, which))
    unread = (*before, *after)
    return pl.pallas_call(
        without(add_kernel, 2, unread),
        out_shape=jax.ShapeDtypeStruct(ours.shape, jnp.bfloat16),
        grid=(pairs,),
        in_specs=[side, block] + [pl.BlockSpec(memory_space=pl.ANY)] * len(unread),
        out_specs=side,
        input_output_aliases={2: 0} if before else {},
        compiler_params=pltpu.CompilerParams(vmem_limit_bytes=SMALL_LIMIT),
        cost_estimate=pl.CostEstimate(
            flops=nodes * pairs * pair_rows * width,
            bytes_accessed=6 * nodes * pairs * pair_rows * width,
            transcendentals=0,
        ),
    )(ours, theirs, *unread)


def update_kernel(place_ref, owner_ref, new_ref, blocks_ref, first_ref, second_ref, send_ref, total, firsts, seconds):
    nodes = send_ref.shape[0]
    experts, rows, width = first_ref.shape
    pair = pl.program_id(0)
    pairs = pl.num_programs(0)

    def block_of(slot):
        position = place_ref[slot]
        both = blocks_ref[position // 2].astype(jnp.float32)
        return jnp.where(position % 2 == 1, both[rows:], both[:rows])

    @pl.when(pair == 0)
    def _():
        @pl.loop(0, experts, unroll=4)
        def _(expert):
            total[expert] = block_of(expert)

        @pl.loop(0, owner_ref.shape[0])
        def _(slot):
            expert = owner_ref[slot]
            total[expert] = total[expert] + block_of(experts + slot)

        @pl.loop(0, experts, unroll=4)
        def _(expert):
            first, second = moments(first_ref[expert], second_ref[expert], total[expert])
            firsts[expert] = first
            seconds[expert] = second

        for array in (firsts, seconds):
            array[experts] = jnp.zeros((rows, width), jnp.float32)

    for node in range(nodes):
        place = (node * pairs + pair) * 2
        left, right = new_ref[place], new_ref[place + 1]
        for which, array in enumerate((firsts, seconds)):
            both = jnp.concatenate([array[left], array[right]], axis=0)
            send_ref[node, which, 0] = both.astype(jnp.bfloat16)


def update_call(blocks, old_place, old_owner, new_table, first, second):
    nodes, pairs, pair_rows, columns = blocks.shape
    experts, rows, _ = first.shape
    whole = pl.BlockSpec(first.shape, lambda i, *_: (0, 0, 0))
    return pl.pallas_call(
        update_kernel,
        out_shape=jax.ShapeDtypeStruct((nodes, 2, pairs, pair_rows, columns), jnp.bfloat16),
        grid_spec=pltpu.PrefetchScalarGridSpec(
            num_scalar_prefetch=3,
            grid=(pairs,),
            in_specs=[
                pl.BlockSpec((nodes * pairs, pair_rows, columns), lambda i, *_: (0, 0, 0)),
                whole,
                whole,
            ],
            out_specs=pl.BlockSpec((nodes, 2, 1, pair_rows, columns), lambda i, *_: (0, 0, i, 0, 0)),
            scratch_shapes=[
                pltpu.VMEM((experts, rows, columns), jnp.float32),
                pltpu.VMEM((experts + 1, rows, columns), jnp.float32),
                pltpu.VMEM((experts + 1, rows, columns), jnp.float32),
            ],
        ),
        compiler_params=pltpu.CompilerParams(vmem_limit_bytes=SMALL_LIMIT),
        cost_estimate=pl.CostEstimate(
            flops=10 * experts * rows * columns,
            bytes_accessed=experts * rows * columns * 8 + 6 * nodes * pairs * pair_rows * columns,
            transcendentals=0,
        ),
    )(old_place, old_owner, new_table, blocks.reshape(nodes * pairs, pair_rows, columns), first, second)


def place_kernel(ahead_ref, got_ref, *out_refs):
    nodes, _, pair_rows, columns = ahead_ref.shape
    rows = pair_rows // 2
    for start in range(0, columns, 128):
        part = slice(start, start + 128)
        first, second = (got_ref[:, which, 0, :, part].astype(jnp.float32) for which in range(2))
        weight = step_weight(ahead_ref[:, 0, :, part].astype(jnp.float32), first, second)
        for out_ref, both in zip(out_refs, (weight, first, second)):
            for side in range(2):
                block = both[:, side * rows : (side + 1) * rows].reshape(nodes * rows, 128)
                out_ref[side, :, part] = block.astype(out_ref.dtype)


def place_call(ahead, got):
    nodes, pairs, pair_rows, columns = ahead.shape
    all_rows = nodes * pair_rows // 2
    return pl.pallas_call(
        place_kernel,
        out_shape=[
            jax.ShapeDtypeStruct((2 * pairs, all_rows, columns), dtype)
            for dtype in (jnp.bfloat16, jnp.float32, jnp.float32)
        ],
        grid=(pairs,),
        in_specs=[
            pl.BlockSpec((nodes, 1, pair_rows, columns), lambda i: (0, i, 0, 0)),
            pl.BlockSpec((nodes, 2, 1, pair_rows, columns), lambda i: (0, 0, i, 0, 0)),
        ],
        out_specs=[pl.BlockSpec((2, all_rows, columns), lambda i: (i, 0, 0))] * 3,
        compiler_params=pltpu.CompilerParams(vmem_limit_bytes=SMALL_LIMIT),
        cost_estimate=pl.CostEstimate(
            flops=20 * nodes * pairs * pair_rows * columns,
            bytes_accessed=16 * nodes * pairs * pair_rows * columns,
            transcendentals=0,
        ),
    )(ahead, got)


def exchange(array):
    return lax.all_to_all(array, "node", split_axis=0, concat_axis=0, tiled=True)


def paired(
    master_weight, first_moment, second_moment, features, grad_out, old_place, new_place, old_owner, new_owner, new_table
):
    nodes = lax.axis_size("node")
    side = jnp.reshape(lax.axis_index("local").astype(jnp.int32), (1,))
    ahead, *theirs = front_call(nodes, side, new_place, new_owner, features, grad_out, master_weight)
    ahead = exchange(ahead)
    ours = gradient_call(nodes, side, features, grad_out, (*theirs, new_table))
    low, high = (lax.ppermute(part, "local", [(0, 1), (1, 0)]) for part in theirs)
    blocks = add_call(0, ours, low)
    blocks = exchange(add_call(7, ours, high, (blocks,), (arrived_call(ahead),)))
    send = update_call(blocks, old_place, old_owner, new_table, first_moment, second_moment)
    return tuple(place_call(ahead, exchange(send)))


def plain(
    master_weight, first_moment, second_moment, features, grad_out, old_table, new_table
):
    nodes = lax.axis_size("node")
    capacity = features.shape[0]
    experts, rows, columns = master_weight.shape
    slot_grad = jnp.einsum("cltr,cltf->crf", features, grad_out, preferred_element_type=jnp.float32)
    part = lax.psum_scatter(
        slot_grad.astype(jnp.bfloat16), "local", scatter_dimension=2, tiled=True
    )
    part = part.reshape(capacity, nodes, rows, columns).transpose(1, 0, 2, 3)
    blocks = exchange(part).reshape(nodes * capacity, rows, columns).astype(jnp.float32)
    gradient = jnp.zeros((experts + 1, rows, columns), jnp.float32).at[old_table].add(blocks)[:experts]
    got = []
    for array in (master_weight, *moments(first_moment, second_moment, gradient)):
        padded = jnp.concatenate([array.astype(jnp.bfloat16), jnp.zeros((1, rows, columns), jnp.bfloat16)])
        sent = exchange(padded[new_table].reshape(nodes, capacity, rows, columns))
        sent = sent.transpose(1, 0, 2, 3).reshape(capacity, nodes * rows, columns)
        got.append(sent.astype(jnp.float32))
    return step_weight(*got).astype(jnp.bfloat16), got[1], got[2]


def local(
    master_weight,
    first_moment,
    second_moment,
    features,
    grad_out,
    old_place,
    new_place,
    old_owner,
    new_owner,
):
    nodes = lax.axis_size("node")
    capacity = features.shape[0]
    experts, rows, columns = master_weight.shape
    positions = nodes * capacity
    primaries = jnp.arange(experts, dtype=jnp.int32)
    new_table = position_table(new_place, jnp.concatenate([primaries, new_owner]), positions, experts)
    state = (master_weight, first_moment, second_moment, features, grad_out)
    if (
        lax.axis_size("local") == 2
        and capacity % 2 == 0
        and rows % 8 == 0
        and experts % 4 == 0
        and columns % 1024 == 0
    ):
        return paired(*state, old_place, new_place, old_owner, new_owner, new_table)
    old_table = position_table(old_place, jnp.concatenate([primaries, old_owner]), positions, experts)
    return plain(*state, old_table, new_table)


def solution(mesh):
    return jax.shard_map(
        local,
        mesh=mesh,
        in_specs=(
            P(None, "node", "local"),
            P(None, "node", "local"),
            P(None, "node", "local"),
            P("node", "local", None, None),
            P("node", "local", None, None),
            P(),
            P(),
            P(),
            P(),
        ),
        out_specs=(P("node", None, "local"), P("node", None, "local"), P("node", None, "local")),
        check_vma=False,
    )
```
